32 devices in a mesh: kgrp: 8 (over y, x, core), pts: 4 (over z).
Axes of the slice: x: 2, y: 2, z: 4, core: 2. Of those that a mesh axis runs over, the one named last changes fastest.
Arguments:
- vectors: bfloat16 [32, 32, 2048], P('kgrp'), may hold values from -6 to 6
- psi_val: bfloat16 [32, 48, 2048], P('kgrp', None, 'pts'), may hold values from -1.1953125 to 1.1953125
- psi_con: bfloat16 [32, 96, 2048], P('kgrp', None, 'pts'), may hold values from -1.1953125 to 1.1953125
- val_count: int32 [32], P('kgrp'), may hold values from 8 to 32, as said below
- con_count: int32 [32], P('kgrp'), may hold values from 16 to 64, as said below
- val_offset: int32 [32], P('kgrp'), may hold values from 0 to 16
- con_offset: int32 [32], P('kgrp'), may hold values from 0 to 32
- screening: bfloat16 [32, 2048, 2048], P('kgrp', 'pts'), may hold values from -0.0234375 to 0.0234375
- q_table: int32 [32, 32], replicated, may hold values from 0 to 31, as said below
Outputs:
- kernel_image: bfloat16 [32, 32, 2048], P('kgrp', None, 'pts')
The draws below stay inside these ranges and needn't reach their ends.
Inputs may be any that keep to these rules, and one draw needn't show every extreme that they name: `val_count`: at least one k-point has a full window of 32 valence bands. `con_count`: at least one k-point has a full window of 64 conduction bands. q_table[k, k'] = (label_k - label_k') mod 32 for a permutation label of 0 to 31, so every row and every column holds each q once.
All inputs are finite; a program needn't handle non-finite values.
Results may differ from the reference program's by a relative error of at most 0.023.
Values may be sent and summed in bfloat16 or wider, within the bound.
A program may use at most 64 MiB of HBM per device.

```python
import jax
import jax.numpy as jnp
from jax import lax

INTERP_POINTS = 2048
NV = 32
NC = 64
VB = 48
CB = 96
TRIAL_VECTORS = 32
KPOINT_COUNT = 32


def window_counts(key, most):
    counts = jax.random.randint(key, (KPOINT_COUNT,), most // 4, most + 1)
    where = jax.random.randint(jax.random.fold_in(key, 7), (), 0, KPOINT_COUNT)
    return counts.at[where].set(most).astype(jnp.int32)


def draw_val_count(key, part):
    return window_counts(jax.random.fold_in(key, 11), NV)


def draw_con_count(key, part):
    return window_counts(jax.random.fold_in(key, 13), NC)


def draw_q_table(key, part):
    labels = jax.random.permutation(jax.random.fold_in(key, 17), KPOINT_COUNT).astype(jnp.int32)
    return ((labels[:, None] - labels[None, :]) % KPOINT_COUNT).astype(jnp.int32)


def with_ends(array, key, least, top_value):
    extent = array.shape
    place = [jax.random.randint(jax.random.fold_in(key, axis), (), 0, extent[axis]) for axis in range(len(extent))]
    array = array.at[tuple(place)].set(least)
    longest = extent.index(max(extent))
    place[longest] = (place[longest] + 1) % extent[longest]
    return array.at[tuple(place)].set(top_value)


def steps_of(key, extent, cuts, least, high):
    loudness, own = 1.0, jax.random.fold_in(key, 6)
    for dim, parts in cuts:
        heights = jnp.exp(jax.random.uniform(jax.random.fold_in(own, dim), (parts,), jnp.float32, least / len(cuts), high / len(cuts)))
        loudness = loudness * jnp.repeat(heights, extent[dim] // parts).reshape([-1 if axis == dim else 1 for axis in range(len(extent))])
    return loudness


def normal_values(rng, dims, spread, limit, split=(), held_as=jnp.bfloat16):
    drawn = spread * jax.random.normal(rng, dims, jnp.float32)
    if split:
        drawn = drawn * steps_of(rng, dims, split, -0.22, 0.18)
    return jnp.clip(drawn, -limit, limit).astype(held_as)


def setup_inputs(seed: int = 0) -> dict:
    arg_keys = jax.random.split(jax.random.key(seed), 10)
    vectors = normal_values(arg_keys[0], (KPOINT_COUNT, TRIAL_VECTORS, NV * NC), 1.0, 6.0, ((0, 8),))
    psi_val = normal_values(arg_keys[1], (KPOINT_COUNT, VB, INTERP_POINTS), 0.2, 1.1953125, ((0, 8), (2, 4)))
    psi_con = normal_values(arg_keys[2], (KPOINT_COUNT, CB, INTERP_POINTS), 0.2, 1.1953125, ((0, 8), (2, 4)))
    val_count = draw_val_count(jax.random.fold_in(arg_keys[9], 71), 0)
    con_count = draw_con_count(jax.random.fold_in(arg_keys[9], 71), 0)
    val_offset = with_ends(jax.random.randint(arg_keys[5], (KPOINT_COUNT,), 0, VB - NV + 1), jax.random.fold_in(arg_keys[5], 1), 0, VB - NV).astype(jnp.int32)
    con_offset = with_ends(jax.random.randint(arg_keys[6], (KPOINT_COUNT,), 0, CB - NC + 1), jax.random.fold_in(arg_keys[6], 1), 0, CB - NC).astype(jnp.int32)
    screening = normal_values(arg_keys[7], (KPOINT_COUNT, INTERP_POINTS, INTERP_POINTS), (INTERP_POINTS * KPOINT_COUNT) ** -0.5, 0.0234375, ((0, 8), (1, 4)))
    q_table = draw_q_table(jax.random.fold_in(arg_keys[9], 71), 0)
    return dict(vectors=vectors, psi_val=psi_val, psi_con=psi_con, val_count=val_count, con_count=con_count, val_offset=val_offset, con_offset=con_offset, screening=screening, q_table=q_table)


def pair_window(psi_v, psi_c, count_v, count_c, start_v, start_c):
    win_v = lax.dynamic_slice_in_dim(psi_v, start_v.astype(jnp.int32), NV, 0).astype(jnp.float32)
    win_c = lax.dynamic_slice_in_dim(psi_c, start_c.astype(jnp.int32), NC, 0).astype(jnp.float32)
    keep_v = (jnp.arange(NV, dtype=jnp.int32) < count_v).astype(jnp.float32)
    keep_c = (jnp.arange(NC, dtype=jnp.int32) < count_c).astype(jnp.float32)
    left = win_v * keep_v[:, None]
    right = win_c * keep_c[:, None]
    prod = left[:, None, :] * right[None, :, :]
    return prod.reshape(NV * NC, prod.shape[-1]).astype(jnp.bfloat16)


def reference(vectors, psi_val, psi_con, val_count, con_count, val_offset, con_offset, screening, q_table):
    kpoint_index = jnp.arange(KPOINT_COUNT, dtype=jnp.int32)

    def zeta_of(k):
        return pair_window(psi_val[k], psi_con[k], val_count[k], con_count[k], val_offset[k], con_offset[k])

    def project_density(k):
        return jnp.dot(vectors[k], zeta_of(k), preferred_element_type=jnp.float32).astype(jnp.bfloat16)

    projected_pair = lax.map(project_density, kpoint_index)

    def shift_by_transfer(mapped_output, q):
        matching_entry = (q_table == q).astype(jnp.int32)
        sender_kpoint = jnp.sum(matching_entry * kpoint_index[None, :], axis=1).astype(jnp.int32)
        picked = projected_pair[sender_kpoint].astype(jnp.float32)
        block = screening[q].astype(jnp.float32)
        return mapped_output + jnp.einsum('cbv,mv->cbm', picked, block), None

    mapped_output, unused_slot = lax.scan(shift_by_transfer, jnp.zeros((KPOINT_COUNT, TRIAL_VECTORS, INTERP_POINTS), jnp.float32), kpoint_index)
    home = mapped_output.astype(jnp.bfloat16)

    def return_trip(k):
        return jnp.dot(home[k], zeta_of(k).T, preferred_element_type=jnp.float32).astype(jnp.bfloat16)

    return lax.map(return_trip, kpoint_index)
```

```python
import functools

import jax
import jax.numpy as jnp
from jax import lax
from jax.experimental import pallas as pl
from jax.experimental.pallas import tpu as pltpu
from jax.sharding import PartitionSpec as P

NV = 32
NC = 64
MESH = pl.DeviceIdType.MESH
VMEM_BYTES = 60 * 1024 * 1024


def flip(o, d):
    out, bit = o, 1
    while bit <= d:
        if d & bit:
            out = out + bit - 2 * bit * ((o // bit) % 2)
        bit *= 2
    return out


def last_hop(d, i, count):
    low = d & -d
    high = 1 << (d.bit_length() - 1)
    return low if 2 * i < count else high


def nearest(z, i, count):
    far = (2 * z) // count
    zz = z + far * (count - 1 - 2 * z)
    step = (i + 1) // 2
    t = jnp.where(i <= 2 * zz, zz + (step if i % 2 else -step), i)
    return t + far * (count - 1 - 2 * t)


def kernel(
    groups, points,
    val_count, con_count, val_offset, con_offset, sender,
    vectors, psi_val, psi_con, screening, out,
    w_buf, zeta, piece, res, s1, r1, s2, r2, mine, s3, r3, mine3,
    w_sem, ag_send, ag_recv, s1_send, s1_recv, s2_send, s2_recv, s3_send, s3_recv,
):
    k_local, trials, slots = vectors.shape
    m_local = psi_val.shape[2]
    q_local = w_buf.shape[0]
    rows = k_local * trials
    outer = groups // 2
    p_local = slots // points
    g = lax.axis_index("kgrp")
    z = lax.axis_index("pts")
    o, c = g // 2, g % 2
    sibling = g + 1 - 2 * c

    barrier = pltpu.get_barrier_semaphore()
    partners = [(sibling, z)]
    partners += [(flip(o, d) * 2 + c, z) for d in range(1, outer)]
    partners += [(g, (z + t) % points) for t in range(1, points)]
    for who in partners:
        pl.semaphore_signal(barrier, inc=1, device_id=who, device_id_type=MESH)

    w_copy = pltpu.make_async_copy(screening, w_buf, w_sem)
    w_copy.start()

    my_rows = pl.multiple_of(g * rows, rows)

    def project(j, carry):
        def select(count, offset, n, held):
            at = lax.broadcasted_iota(jnp.int32, (n, held), 0)
            src = lax.broadcasted_iota(jnp.int32, (n, held), 1)
            hit = (src == at + offset) & (at < count)
            return jnp.where(hit, 1.0, 0.0).astype(jnp.bfloat16)

        left = jnp.dot(
            select(val_count[j], val_offset[j], NV, psi_val.shape[1]), psi_val[j],
            preferred_element_type=jnp.float32,
        )
        right = jnp.dot(
            select(con_count[j], con_offset[j], NC, psi_con.shape[1]), psi_con[j],
            preferred_element_type=jnp.float32,
        )
        for v in range(NV):
            zeta[j, v * NC : (v + 1) * NC, :] = (left[v : v + 1, :] * right).astype(jnp.bfloat16)
        local = jnp.dot(vectors[j], zeta[j], preferred_element_type=jnp.float32)
        at = pl.multiple_of(g * rows + j * trials, trials)
        piece[z, pl.ds(at, trials), :] = local.astype(jnp.bfloat16)
        return carry

    lax.fori_loop(0, k_local, project, 0)
    pl.semaphore_wait(barrier, len(partners))

    pending = []

    def block(group, zp):
        return piece.at[zp, pl.ds(pl.multiple_of(group * rows, rows), rows), :]

    def ag_copy(group, zp, slot, index, who):
        return pltpu.make_async_remote_copy(
            src_ref=block(group, zp),
            dst_ref=block(group, zp),
            send_sem=ag_send.at[index],
            recv_sem=ag_recv.at[slot[0], slot[1], zp],
            device_id=who,
            device_id_type=MESH,
        )

    sent = [0]

    def send(group, zp, slot, who):
        copy = ag_copy(group, zp, slot, sent[0], who)
        sent[0] += 1
        copy.start()
        pending.append(copy)

    def arrived(group, zp, slot):
        ag_copy(group, zp, slot, 0, (g, z)).wait_recv()

    order = [nearest(z, i, points) if i else z for i in range(points)]

    def forward(d, i):
        group = flip(o, d) * 2 + c
        bit = 1
        while bit < outer:
            if not d & bit and last_hop(d | bit, i, points) == bit:
                send(group, order[i], (d | bit, 0), (flip(o, bit) * 2 + c, z))
            bit *= 2
        send(group, order[i], (d, 1), (sibling, z))

    def take(d, i):
        arrived(flip(o, d) * 2 + c, order[i], (d, 0))
        forward(d, i)

    def product(d):
        base = pl.multiple_of(flip(o, d) * 2 * rows, 2 * rows)
        for i in range(points):
            arrived(flip(o, d) * 2 + 1 - c, order[i], (d, 1))

        def one(q, carry):
            lhs = jnp.concatenate([piece[t, pl.ds(base, 2 * rows), :] for t in range(points)], axis=1)
            got = lax.dot_general(
                lhs, w_buf[q], (((1,), (1,)), ((), ())), preferred_element_type=jnp.float32
            )
            res[q, pl.ds(flip(o, d) * 2 * k_local, 2 * k_local)] = got.reshape(2 * k_local, trials, m_local)
            return carry

        lax.fori_loop(0, q_local, one, 0)

    near = [d for d in range(1, outer) if d & (d - 1) == 0]
    far = [d for d in range(1, outer) if d & (d - 1)]
    far.sort(key=lambda d: bin(d).count("1"))
    for i in range(1, points):
        t = nearest(z, i, points)
        send(g, z, (0, 0), (g, t))
    forward(0, 0)
    for i in range(1, points):
        take(0, i)
        for d in near:
            take(d, i - 1)
    for d in near:
        take(d, points - 1)
    w_copy.wait()
    product(0)
    ready = near[:]
    for d in far:
        for i in range(points):
            take(d, i)
            if 2 * i + 2 == points and ready:
                product(ready.pop(0))
        while ready and d == far[-1]:
            product(ready.pop(0))
    while ready:
        product(ready.pop(0))
    for d in far:
        product(d)

    def gathered(group, j):
        k = group * k_local + j
        total = None
        for q in range(q_local):
            term = res[q, sender[q, k]]
            total = term if total is None else total + term
        return total

    first, second, third = [], [], []
    for j in range(k_local):
        for d in range(outer):
            s1[j, d] = gathered(flip(o, d) * 2 + 1 - c, j).astype(jnp.bfloat16)
        copy = pltpu.make_async_remote_copy(
            src_ref=s1.at[j], dst_ref=r1.at[j],
            send_sem=s1_send.at[j], recv_sem=s1_recv.at[j],
            device_id=(sibling, z), device_id_type=MESH,
        )
        copy.start()
        first.append(copy)
    for j in range(k_local):
        sums = [gathered(flip(o, d) * 2 + c, j) for d in range(outer)]
        first[j].wait_recv()
        mine[j] = sums[0] + r1[j, 0].astype(jnp.float32)
        copies = []
        for d in range(outer - 1, 0, -1):
            s2[j, d] = (sums[d] + r1[j, d].astype(jnp.float32)).astype(jnp.bfloat16)
            copy = pltpu.make_async_remote_copy(
                src_ref=s2.at[j, d], dst_ref=r2.at[j, d],
                send_sem=s2_send.at[j, d], recv_sem=s2_recv.at[j, d],
                device_id=(flip(o, d) * 2 + c, z), device_id_type=MESH,
            )
            copy.start()
            copies.append((d, copy))
        second.append(copies)
    for j in range(k_local):
        total = mine[j]
        for d, copy in second[j]:
            copy.wait_recv()
            total = total + r2[j, d].astype(jnp.float32)
        home = total.astype(jnp.bfloat16)

        def back(t, carry):
            at = pl.multiple_of(t * p_local, p_local)
            mine3[j, t] = lax.dot_general(
                home, zeta[j, pl.ds(at, p_local), :], (((1,), (1,)), ((), ())),
                preferred_element_type=jnp.float32,
            )
            s3[j, t] = mine3[j, t].astype(jnp.bfloat16)
            return carry

        lax.fori_loop(0, points, back, 0)
        copies = []
        for t in range(points - 1, 0, -1):
            to = (z + t) % points
            copy = pltpu.make_async_remote_copy(
                src_ref=s3.at[j, to], dst_ref=r3.at[j, t],
                send_sem=s3_send.at[j, t], recv_sem=s3_recv.at[j, t],
                device_id=(g, to), device_id_type=MESH,
            )
            copy.start()
            copies.append((t, copy))
        third.append(copies)
    for j in range(k_local):
        total = mine3[j, z]
        for t, copy in third[j]:
            copy.wait_recv()
            total = total + r3[j, t].astype(jnp.float32)
        out[j] = total.astype(jnp.bfloat16)
    for copy in pending:
        copy.wait_send()
    for j in range(k_local):
        first[j].wait_send()
        for d, copy in second[j] + third[j]:
            copy.wait_send()


def shards(
    groups, points,
    vectors, psi_val, psi_con, val_count, con_count, val_offset, con_offset, screening, q_table,
):
    k_local, trials, slots = vectors.shape
    k_total = q_table.shape[0]
    q_local, m_local, m_total = screening.shape
    outer = groups // 2
    p_local = slots // points
    rows = k_local * trials
    owned = lax.axis_index("kgrp") * q_local + jnp.arange(q_local, dtype=jnp.int32)
    match = (q_table[None, :, :] == owned[:, None, None]).astype(jnp.int32)
    sender = jnp.sum(match * jnp.arange(k_total, dtype=jnp.int32)[None, None, :], axis=2)
    sender = jnp.minimum(sender, k_total - 1)
    smem = pl.BlockSpec(memory_space=pltpu.SMEM)
    vmem = pl.BlockSpec(memory_space=pltpu.VMEM)
    bf16, f32 = jnp.bfloat16, jnp.float32
    dma = pltpu.SemaphoreType.DMA
    flops = 2 * k_total * trials * q_local * m_local * m_total
    return pl.pallas_call(
        functools.partial(kernel, groups, points),
        out_shape=jax.ShapeDtypeStruct((k_local, trials, p_local), bf16),
        in_specs=[smem] * 5 + [vmem] * 3 + [pl.BlockSpec(memory_space=pl.ANY)],
        out_specs=vmem,
        scratch_shapes=[
            pltpu.VMEM((q_local, m_local, m_total), bf16),
            pltpu.VMEM((k_local, slots, m_local), bf16),
            pltpu.VMEM((points, groups * rows, m_local), bf16),
            pltpu.VMEM((q_local, groups * k_local, trials, m_local), f32),
            pltpu.VMEM((k_local, outer, trials, m_local), bf16),
            pltpu.VMEM((k_local, outer, trials, m_local), bf16),
            pltpu.VMEM((k_local, outer, trials, m_local), bf16),
            pltpu.VMEM((k_local, outer, trials, m_local), bf16),
            pltpu.VMEM((k_local, trials, m_local), f32),
            pltpu.VMEM((k_local, points, trials, p_local), bf16),
            pltpu.VMEM((k_local, points, trials, p_local), bf16),
            pltpu.VMEM((k_local, points, trials, p_local), f32),
            dma,
            dma((groups * points,)),
            dma((outer, 2, points)),
            dma((k_local,)),
            dma((k_local,)),
            dma((k_local, outer)),
            dma((k_local, outer)),
            dma((k_local, points)),
            dma((k_local, points)),
        ],
        compiler_params=pltpu.CompilerParams(
            collective_id=0, has_side_effects=True, vmem_limit_bytes=VMEM_BYTES
        ),
        cost_estimate=pl.CostEstimate(flops=flops, bytes_accessed=screening.size * 2, transcendentals=0),
    )(
        val_count, con_count, val_offset, con_offset, sender,
        vectors, psi_val, psi_con, screening,
    )


def solution(mesh):
    placed = (
        P("kgrp", None, None),
        P("kgrp", None, "pts"),
        P("kgrp", None, "pts"),
        P("kgrp"),
        P("kgrp"),
        P("kgrp"),
        P("kgrp"),
        P("kgrp", "pts", None),
        P(),
    )
    return jax.shard_map(
        functools.partial(shards, mesh.shape["kgrp"], mesh.shape["pts"]),
        mesh=mesh, in_specs=placed, out_specs=P("kgrp", None, "pts"), check_vma=False,
    )
```

```python
import functools

import jax
import jax.numpy as jnp
from jax import lax
from jax.experimental import pallas as pl
from jax.experimental.pallas import tpu as pltpu
from jax.sharding import PartitionSpec as P

NV = 32
NC = 64
MESH = pl.DeviceIdType.MESH
VMEM_BYTES = 60 * 1024 * 1024


def flip(o, d):
    out, bit = o, 1
    while bit <= d:
        if d & bit:
            out = out + bit - 2 * bit * ((o // bit) % 2)
        bit *= 2
    return out


def last_hop(d, i, count):
    low = d & -d
    high = 1 << (d.bit_length() - 1)
    return low if 2 * i < count else high


def nearest(z, i, count):
    far = (2 * z) // count
    zz = z + far * (count - 1 - 2 * z)
    step = (i + 1) // 2
    t = jnp.where(i <= 2 * zz, zz + (step if i % 2 else -step), i)
    return t + far * (count - 1 - 2 * t)


def kernel(
    groups, points, halves,
    val_count, con_count, val_offset, con_offset, sender,
    vectors, psi_val, psi_con, screening, out,
    w_buf, zeta, piece, res, s1, r1, s2, r2, mine, s3, r3, mine3,
    w_sem, ag_send, ag_recv, s1_send, s1_recv, s2_send, s2_recv, s3_send, s3_recv,
):
    k_local, trials, slots = vectors.shape
    m_local = psi_val.shape[2]
    q_local = w_buf.shape[0]
    rows = k_local * trials
    outer = groups // 2
    p_local = slots // points
    g = lax.axis_index("kgrp")
    z = lax.axis_index("pts")
    o, c = g // 2, g % 2
    sibling = g + 1 - 2 * c

    barrier = pltpu.get_barrier_semaphore()
    partners = [(sibling, z)]
    partners += [(flip(o, d) * 2 + c, z) for d in range(1, outer)]
    partners += [(g, (z + t) % points) for t in range(1, points)]
    for who in partners:
        pl.semaphore_signal(barrier, inc=1, device_id=who, device_id_type=MESH)

    w_copy = pltpu.make_async_copy(screening, w_buf, w_sem)
    w_copy.start()

    def project(j, carry):
        def select(count, offset, n, held):
            at = lax.broadcasted_iota(jnp.int32, (n, held), 0)
            src = lax.broadcasted_iota(jnp.int32, (n, held), 1)
            hit = (src == at + offset) & (at < count)
            return jnp.where(hit, 1.0, 0.0).astype(jnp.bfloat16)

        left = jnp.dot(
            select(val_count[j], val_offset[j], NV, psi_val.shape[1]), psi_val[j],
            preferred_element_type=jnp.float32,
        )
        right = jnp.dot(
            select(con_count[j], con_offset[j], NC, psi_con.shape[1]), psi_con[j],
            preferred_element_type=jnp.float32,
        )
        for v in range(NV):
            zeta[j, v * NC : (v + 1) * NC, :] = (left[v : v + 1, :] * right).astype(jnp.bfloat16)
        local = jnp.dot(vectors[j], zeta[j], preferred_element_type=jnp.float32)
        at = pl.multiple_of(g * rows + j * trials, trials)
        piece[z, pl.ds(at, trials), :] = local.astype(jnp.bfloat16)
        return carry

    pending = []

    part = rows // halves

    def block(group, zp, h):
        return piece.at[zp, pl.ds(pl.multiple_of(group * rows + h * part, part), part), :]

    def ag_copy(group, zp, slot, index, who):
        return pltpu.make_async_remote_copy(
            src_ref=block(group, zp, slot[2]),
            dst_ref=block(group, zp, slot[2]),
            send_sem=ag_send.at[index],
            recv_sem=ag_recv.at[slot[0], slot[1], slot[2], zp],
            device_id=who,
            device_id_type=MESH,
        )

    sent = [0]

    def send(group, zp, slot, who):
        copy = ag_copy(group, zp, slot, sent[0], who)
        sent[0] += 1
        copy.start()
        pending.append(copy)

    def arrived(group, zp, slot):
        ag_copy(group, zp, slot, 0, (g, z)).wait_recv()

    order = [nearest(z, i, points) if i else z for i in range(points)]

    def forward(d, i, h):
        group = flip(o, d) * 2 + c
        bit = 1
        while bit < outer:
            if not d & bit and last_hop(d | bit, i, points) == bit:
                send(group, order[i], (d | bit, 0, h), (flip(o, bit) * 2 + c, z))
            bit *= 2
        send(group, order[i], (d, 1, h), (sibling, z))

    def take(d, i, h):
        arrived(flip(o, d) * 2 + c, order[i], (d, 0, h))
        forward(d, i, h)

    def product(d):
        base = pl.multiple_of(flip(o, d) * 2 * rows, 2 * rows)
        for i in range(points):
            for h in range(halves):
                arrived(flip(o, d) * 2 + 1 - c, order[i], (d, 1, h))

        def one(q, carry):
            lhs = jnp.concatenate([piece[t, pl.ds(base, 2 * rows), :] for t in range(points)], axis=1)
            got = lax.dot_general(
                lhs, w_buf[q], (((1,), (1,)), ((), ())), preferred_element_type=jnp.float32
            )
            res[q, pl.ds(flip(o, d) * 2 * k_local, 2 * k_local)] = got.reshape(2 * k_local, trials, m_local)
            return carry

        lax.fori_loop(0, q_local, one, 0)

    near = [d for d in range(1, outer) if d & (d - 1) == 0]
    far = [d for d in range(1, outer) if d & (d - 1)]
    far.sort(key=lambda d: bin(d).count("1"))
    each = k_local // halves
    for h in range(halves):
        lax.fori_loop(h * each, (h + 1) * each, project, 0)
        if h == 0:
            pl.semaphore_wait(barrier, len(partners))
        for i in range(1, points):
            send(g, z, (0, 0, h), (g, order[i]))
        forward(0, 0, h)
    expected = [(i + 1.5 * h, 0, i, h) for h in range(halves) for i in range(1, points)]
    expected += [
        (i + 1.5 * h + 0.9, d, i, h) for h in range(halves) for i in range(points) for d in near
    ]
    for when, d, i, h in sorted(expected):
        take(d, i, h)
    w_copy.wait()
    product(0)
    ready = near[:]
    for d in far:
        for h in range(halves):
            for i in range(points):
                take(d, i, h)
            if h == 0 and ready:
                product(ready.pop(0))
    while ready:
        product(ready.pop(0))
    for d in far:
        product(d)

    def gathered(group, j):
        k = group * k_local + j
        total = None
        for q in range(q_local):
            term = res[q, sender[q, k]]
            total = term if total is None else total + term
        return total

    first, second, third = [], [], []
    for j in range(k_local):
        for d in range(outer):
            s1[j, d] = gathered(flip(o, d) * 2 + 1 - c, j).astype(jnp.bfloat16)
        copy = pltpu.make_async_remote_copy(
            src_ref=s1.at[j], dst_ref=r1.at[j],
            send_sem=s1_send.at[j], recv_sem=s1_recv.at[j],
            device_id=(sibling, z), device_id_type=MESH,
        )
        copy.start()
        first.append(copy)
    for j in range(k_local):
        sums = [gathered(flip(o, d) * 2 + c, j) for d in range(outer)]
        first[j].wait_recv()
        mine[j] = sums[0] + r1[j, 0].astype(jnp.float32)
        copies = []
        for d in range(outer - 1, 0, -1):
            s2[j, d] = (sums[d] + r1[j, d].astype(jnp.float32)).astype(jnp.bfloat16)
            copy = pltpu.make_async_remote_copy(
                src_ref=s2.at[j, d], dst_ref=r2.at[j, d],
                send_sem=s2_send.at[j, d], recv_sem=s2_recv.at[j, d],
                device_id=(flip(o, d) * 2 + c, z), device_id_type=MESH,
            )
            copy.start()
            copies.append((d, copy))
        second.append(copies)
    for j in range(k_local):
        total = mine[j]
        for d, copy in second[j]:
            copy.wait_recv()
            total = total + r2[j, d].astype(jnp.float32)
        home = total.astype(jnp.bfloat16)

        def back(t, carry):
            at = pl.multiple_of(t * p_local, p_local)
            mine3[j, t] = lax.dot_general(
                home, zeta[j, pl.ds(at, p_local), :], (((1,), (1,)), ((), ())),
                preferred_element_type=jnp.float32,
            )
            s3[j, t] = mine3[j, t].astype(jnp.bfloat16)
            return carry

        lax.fori_loop(0, points, back, 0)
        copies = []
        for t in range(points - 1, 0, -1):
            to = (z + t) % points
            copy = pltpu.make_async_remote_copy(
                src_ref=s3.at[j, to], dst_ref=r3.at[j, t],
                send_sem=s3_send.at[j, t], recv_sem=s3_recv.at[j, t],
                device_id=(g, to), device_id_type=MESH,
            )
            copy.start()
            copies.append((t, copy))
        third.append(copies)
    for j in range(k_local):
        total = mine3[j, z]
        for t, copy in third[j]:
            copy.wait_recv()
            total = total + r3[j, t].astype(jnp.float32)
        out[j] = total.astype(jnp.bfloat16)
    for copy in pending:
        copy.wait_send()
    for j in range(k_local):
        first[j].wait_send()
        for d, copy in second[j] + third[j]:
            copy.wait_send()


def shards(
    groups, points,
    vectors, psi_val, psi_con, val_count, con_count, val_offset, con_offset, screening, q_table,
):
    k_local, trials, slots = vectors.shape
    k_total = q_table.shape[0]
    q_local, m_local, m_total = screening.shape
    outer = groups // 2
    p_local = slots // points
    rows = k_local * trials
    halves = 1 if k_local % 2 else 2
    owned = lax.axis_index("kgrp") * q_local + jnp.arange(q_local, dtype=jnp.int32)
    match = (q_table[None, :, :] == owned[:, None, None]).astype(jnp.int32)
    sender = jnp.sum(match * jnp.arange(k_total, dtype=jnp.int32)[None, None, :], axis=2)
    smem = pl.BlockSpec(memory_space=pltpu.SMEM)
    vmem = pl.BlockSpec(memory_space=pltpu.VMEM)
    bf16, f32 = jnp.bfloat16, jnp.float32
    dma = pltpu.SemaphoreType.DMA
    flops = 2 * k_total * trials * q_local * m_local * m_total
    return pl.pallas_call(
        functools.partial(kernel, groups, points, halves),
        out_shape=jax.ShapeDtypeStruct((k_local, trials, p_local), bf16),
        in_specs=[smem] * 5 + [vmem] * 3 + [pl.BlockSpec(memory_space=pl.ANY)],
        out_specs=vmem,
        scratch_shapes=[
            pltpu.VMEM((q_local, m_local, m_total), bf16),
            pltpu.VMEM((k_local, slots, m_local), bf16),
            pltpu.VMEM((points, groups * rows, m_local), bf16),
            pltpu.VMEM((q_local, groups * k_local, trials, m_local), f32),
            pltpu.VMEM((k_local, outer, trials, m_local), bf16),
            pltpu.VMEM((k_local, outer, trials, m_local), bf16),
            pltpu.VMEM((k_local, outer, trials, m_local), bf16),
            pltpu.VMEM((k_local, outer, trials, m_local), bf16),
            pltpu.VMEM((k_local, trials, m_local), f32),
            pltpu.VMEM((k_local, points, trials, p_local), bf16),
            pltpu.VMEM((k_local, points, trials, p_local), bf16),
            pltpu.VMEM((k_local, points, trials, p_local), f32),
            dma,
            dma((groups * points * halves,)),
            dma((outer, 2, halves, points)),
            dma((k_local,)),
            dma((k_local,)),
            dma((k_local, outer)),
            dma((k_local, outer)),
            dma((k_local, points)),
            dma((k_local, points)),
        ],
        compiler_params=pltpu.CompilerParams(
            collective_id=0, has_side_effects=True, vmem_limit_bytes=VMEM_BYTES
        ),
        cost_estimate=pl.CostEstimate(flops=flops, bytes_accessed=screening.size * 2, transcendentals=0),
    )(
        val_count, con_count, val_offset, con_offset, sender,
        vectors, psi_val, psi_con, screening,
    )


def solution(mesh):
    placed = (
        P("kgrp", None, None),
        P("kgrp", None, "pts"),
        P("kgrp", None, "pts"),
        P("kgrp"),
        P("kgrp"),
        P("kgrp"),
        P("kgrp"),
        P("kgrp", "pts", None),
        P(),
    )
    return jax.shard_map(
        functools.partial(shards, mesh.shape["kgrp"], mesh.shape["pts"]),
        mesh=mesh, in_specs=placed, out_specs=P("kgrp", None, "pts"), check_vma=False,
    )
```

```python
import functools

import jax
import jax.numpy as jnp
from jax import lax
from jax.experimental import pallas as pl
from jax.experimental.pallas import tpu as pltpu
from jax.sharding import PartitionSpec as P

NV = 32
NC = 64
MESH = pl.DeviceIdType.MESH
VMEM_BYTES = 60 * 1024 * 1024


def flip(o, d):
    out, bit = o, 1
    while bit <= d:
        if d & bit:
            out = out + bit - 2 * bit * ((o // bit) % 2)
        bit *= 2
    return out


def last_hop(d, i, count):
    low = d & -d
    high = 1 << (d.bit_length() - 1)
    return low if 2 * i < count else high


def nearest(z, i, count):
    far = (2 * z) // count
    zz = z + far * (count - 1 - 2 * z)
    step = (i + 1) // 2
    t = jnp.where(i <= 2 * zz, zz + (step if i % 2 else -step), i)
    return t + far * (count - 1 - 2 * t)


def kernel(
    groups, points,
    val_count, con_count, val_offset, con_offset, sender,
    vectors, psi_val, psi_con, screening, out,
    w_buf, zeta, piece, res, s1, r1, s2, r2, mine, s3, r3, mine3,
    w_sem, ag_send, ag_recv, s1_send, s1_recv, s2_send, s2_recv, s3_send, s3_recv,
):
    k_local, trials, slots = vectors.shape
    m_local = psi_val.shape[2]
    q_local = w_buf.shape[0]
    rows = k_local * trials
    outer = groups // 2
    p_local = slots // points
    g = lax.axis_index("kgrp")
    z = lax.axis_index("pts")
    o, c = g // 2, g % 2
    sibling = g + 1 - 2 * c

    barrier = pltpu.get_barrier_semaphore()
    partners = [(sibling, z)]
    partners += [(flip(o, d) * 2 + c, z) for d in range(1, outer)]
    partners += [(g, (z + t) % points) for t in range(1, points)]
    for who in partners:
        pl.semaphore_signal(barrier, inc=1, device_id=who, device_id_type=MESH)

    w_copy = pltpu.make_async_copy(screening, w_buf, w_sem)
    w_copy.start()

    my_rows = pl.multiple_of(g * rows, rows)

    def project(j, carry):
        def select(count, offset, n, held):
            at = lax.broadcasted_iota(jnp.int32, (n, held), 0)
            src = lax.broadcasted_iota(jnp.int32, (n, held), 1)
            hit = (src == at + offset) & (at < count)
            return jnp.where(hit, 1.0, 0.0).astype(jnp.bfloat16)

        left = jnp.dot(
            select(val_count[j], val_offset[j], NV, psi_val.shape[1]), psi_val[j],
            preferred_element_type=jnp.float32,
        )
        right = jnp.dot(
            select(con_count[j], con_offset[j], NC, psi_con.shape[1]), psi_con[j],
            preferred_element_type=jnp.float32,
        )
        for v in range(NV):
            zeta[j, v * NC : (v + 1) * NC, :] = (left[v : v + 1, :] * right).astype(jnp.bfloat16)
        local = jnp.dot(vectors[j], zeta[j], preferred_element_type=jnp.float32)
        at = pl.multiple_of(g * rows + j * trials, trials)
        piece[z, pl.ds(at, trials), :] = local.astype(jnp.bfloat16)
        return carry

    lax.fori_loop(0, k_local, project, 0)
    pl.semaphore_wait(barrier, len(partners))

    pending = []

    def block(group, zp):
        return piece.at[zp, pl.ds(pl.multiple_of(group * rows, rows), rows), :]

    def ag_copy(group, zp, slot, index, who):
        return pltpu.make_async_remote_copy(
            src_ref=block(group, zp),
            dst_ref=block(group, zp),
            send_sem=ag_send.at[index],
            recv_sem=ag_recv.at[slot[0], slot[1], zp],
            device_id=who,
            device_id_type=MESH,
        )

    sent = [0]

    def send(group, zp, slot, who):
        copy = ag_copy(group, zp, slot, sent[0], who)
        sent[0] += 1
        copy.start()
        pending.append(copy)

    def arrived(group, zp, slot):
        ag_copy(group, zp, slot, 0, (g, z)).wait_recv()

    order = [nearest(z, i, points) if i else z for i in range(points)]

    def forward(d, i):
        group = flip(o, d) * 2 + c
        bit = 1
        while bit < outer:
            if not d & bit and last_hop(d | bit, i, points) == bit:
                send(group, order[i], (d | bit, 0), (flip(o, bit) * 2 + c, z))
            bit *= 2
        send(group, order[i], (d, 1), (sibling, z))

    def take(d, i):
        arrived(flip(o, d) * 2 + c, order[i], (d, 0))
        forward(d, i)

    def product(d):
        base = pl.multiple_of(flip(o, d) * 2 * rows, 2 * rows)
        for i in range(points):
            arrived(flip(o, d) * 2 + 1 - c, order[i], (d, 1))

        def one(q, carry):
            lhs = jnp.concatenate([piece[t, pl.ds(base, 2 * rows), :] for t in range(points)], axis=1)
            got = lax.dot_general(
                lhs, w_buf[q], (((1,), (1,)), ((), ())), preferred_element_type=jnp.float32
            )
            res[q, pl.ds(flip(o, d) * 2 * k_local, 2 * k_local)] = got.reshape(2 * k_local, trials, m_local)
            return carry

        lax.fori_loop(0, q_local, one, 0)

    near = [d for d in range(1, outer) if d & (d - 1) == 0]
    far = [d for d in range(1, outer) if d & (d - 1)]
    far.sort(key=lambda d: bin(d).count("1"))
    for i in range(1, points):
        t = nearest(z, i, points)
        send(g, z, (0, 0), (g, t))
    forward(0, 0)
    for i in range(1, points):
        take(0, i)
        for d in near:
            take(d, i - 1)
    for d in near:
        take(d, points - 1)
    w_copy.wait()
    product(0)
    ready = near[:]
    for d in far:
        for i in range(points):
            take(d, i)
            if 2 * i + 2 == points and ready:
                product(ready.pop(0))
        while ready and d == far[-1]:
            product(ready.pop(0))
    while ready:
        product(ready.pop(0))
    for d in far:
        product(d)

    def gathered(group, j):
        k = group * k_local + j
        total = None
        for q in range(q_local):
            term = res[q, sender[q, k]]
            total = term if total is None else total + term
        return total

    batches, each = mine.shape[0], mine.shape[1]
    first, second, third = [], [], []
    for j in range(batches):
        for d in range(outer):
            for e in range(each):
                s1[j, d, e] = gathered(flip(o, d) * 2 + 1 - c, j * each + e).astype(jnp.bfloat16)
        copy = pltpu.make_async_remote_copy(
            src_ref=s1.at[j], dst_ref=r1.at[j],
            send_sem=s1_send.at[j], recv_sem=s1_recv.at[j],
            device_id=(sibling, z), device_id_type=MESH,
        )
        copy.start()
        first.append(copy)
    for j in range(batches):
        first[j].wait_recv()
        for e in range(each):
            mine[j, e] = gathered(g, j * each + e) + r1[j, 0, e].astype(jnp.float32)
        copies = []
        for d in range(outer - 1, 0, -1):
            for e in range(each):
                own = gathered(flip(o, d) * 2 + c, j * each + e)
                s2[j, d, e] = (own + r1[j, d, e].astype(jnp.float32)).astype(jnp.bfloat16)
            copy = pltpu.make_async_remote_copy(
                src_ref=s2.at[j, d], dst_ref=r2.at[j, d],
                send_sem=s2_send.at[j, d], recv_sem=s2_recv.at[j, d],
                device_id=(flip(o, d) * 2 + c, z), device_id_type=MESH,
            )
            copy.start()
            copies.append((d, copy))
        second.append(copies)
    for j in range(batches):
        total = mine[j]
        for d, copy in second[j]:
            copy.wait_recv()
            total = total + r2[j, d].astype(jnp.float32)
        home = total.astype(jnp.bfloat16)

        def back(t, carry):
            at = pl.multiple_of(t * p_local, p_local)
            for e in range(each):
                got = lax.dot_general(
                    home[e], zeta[j * each + e, pl.ds(at, p_local), :], (((1,), (1,)), ((), ())),
                    preferred_element_type=jnp.float32,
                )
                mine3[j, t, e] = got
                s3[j, t, e] = got.astype(jnp.bfloat16)
            return carry

        lax.fori_loop(0, points, back, 0)
        copies = []
        for t in range(points - 1, 0, -1):
            to = (z + t) % points
            copy = pltpu.make_async_remote_copy(
                src_ref=s3.at[j, to], dst_ref=r3.at[j, t],
                send_sem=s3_send.at[j, t], recv_sem=s3_recv.at[j, t],
                device_id=(g, to), device_id_type=MESH,
            )
            copy.start()
            copies.append((t, copy))
        third.append(copies)
    for j in range(batches):
        total = mine3[j, z]
        for t, copy in third[j]:
            copy.wait_recv()
            total = total + r3[j, t].astype(jnp.float32)
        out[j * each : (j + 1) * each] = total.astype(jnp.bfloat16)
    for copy in pending:
        copy.wait_send()
    for j in range(batches):
        first[j].wait_send()
        for d, copy in second[j] + third[j]:
            copy.wait_send()


def shards(
    groups, points,
    vectors, psi_val, psi_con, val_count, con_count, val_offset, con_offset, screening, q_table,
):
    k_local, trials, slots = vectors.shape
    k_total = q_table.shape[0]
    q_local, m_local, m_total = screening.shape
    outer = groups // 2
    p_local = slots // points
    rows = k_local * trials
    batches = 1 if k_local % 2 else 2
    each = k_local // batches
    owned = lax.axis_index("kgrp") * q_local + jnp.arange(q_local, dtype=jnp.int32)
    match = (q_table[None, :, :] == owned[:, None, None]).astype(jnp.int32)
    sender = jnp.sum(match * jnp.arange(k_total, dtype=jnp.int32)[None, None, :], axis=2)
    sender = jnp.minimum(sender, k_total - 1)
    smem = pl.BlockSpec(memory_space=pltpu.SMEM)
    vmem = pl.BlockSpec(memory_space=pltpu.VMEM)
    bf16, f32 = jnp.bfloat16, jnp.float32
    dma = pltpu.SemaphoreType.DMA
    flops = 2 * k_total * trials * q_local * m_local * m_total
    return pl.pallas_call(
        functools.partial(kernel, groups, points),
        out_shape=jax.ShapeDtypeStruct((k_local, trials, p_local), bf16),
        in_specs=[smem] * 5 + [vmem] * 3 + [pl.BlockSpec(memory_space=pl.ANY)],
        out_specs=vmem,
        scratch_shapes=[
            pltpu.VMEM((q_local, m_local, m_total), bf16),
            pltpu.VMEM((k_local, slots, m_local), bf16),
            pltpu.VMEM((points, groups * rows, m_local), bf16),
            pltpu.VMEM((q_local, groups * k_local, trials, m_local), f32),
            pltpu.VMEM((batches, outer, each, trials, m_local), bf16),
            pltpu.VMEM((batches, outer, each, trials, m_local), bf16),
            pltpu.VMEM((batches, outer, each, trials, m_local), bf16),
            pltpu.VMEM((batches, outer, each, trials, m_local), bf16),
            pltpu.VMEM((batches, each, trials, m_local), f32),
            pltpu.VMEM((batches, points, each, trials, p_local), bf16),
            pltpu.VMEM((batches, points, each, trials, p_local), bf16),
            pltpu.VMEM((batches, points, each, trials, p_local), f32),
            dma,
            dma((groups * points,)),
            dma((outer, 2, points)),
            dma((k_local,)),
            dma((k_local,)),
            dma((k_local, outer)),
            dma((k_local, outer)),
            dma((k_local, points)),
            dma((k_local, points)),
        ],
        compiler_params=pltpu.CompilerParams(
            collective_id=0, has_side_effects=True, vmem_limit_bytes=VMEM_BYTES
        ),
        cost_estimate=pl.CostEstimate(flops=flops, bytes_accessed=screening.size * 2, transcendentals=0),
    )(
        val_count, con_count, val_offset, con_offset, sender,
        vectors, psi_val, psi_con, screening,
    )


def solution(mesh):
    placed = (
        P("kgrp", None, None),
        P("kgrp", None, "pts"),
        P("kgrp", None, "pts"),
        P("kgrp"),
        P("kgrp"),
        P("kgrp"),
        P("kgrp"),
        P("kgrp", "pts", None),
        P(),
    )
    return jax.shard_map(
        functools.partial(shards, mesh.shape["kgrp"], mesh.shape["pts"]),
        mesh=mesh, in_specs=placed, out_specs=P("kgrp", None, "pts"), check_vma=False,
    )
```
